256 devices in a mesh: inner: 32 (over x_lo, z, core), outer: 8 (over x_hi, y).
Axes of the slice: x: 4 (x_hi: 2, x_lo: 2; x = x_hi * 2 + x_lo), y: 4, z: 8, core: 2. Of those that a mesh axis runs over, the one named last changes fastest.
Arguments:
- queries: float32 [8, 28672, 128], P('outer', 'inner'), may hold values from -52 to 52
- keys: float32 [8, 28672, 128], P('outer', 'inner'), may hold values from -8 to 8
- values: float32 [8, 28672, 128], P('outer', 'inner'), may hold values from -14 to 14
- out_grad: float32 [8, 28672, 128], P('outer', 'inner'), may hold values from -6 to 6
- stretch_order: int32 [8, 224], P('outer', 'inner'), may hold values from 0 to 6, as said below
Outputs:
- attn_out: float32 [8, 28672, 128], P('outer', 'inner')
- query_grad: float32 [8, 28672, 128], P('outer', 'inner')
- key_grad: float32 [8, 28672, 128], P('outer', 'inner')
- value_grad: float32 [8, 28672, 128], P('outer', 'inner')
The draws below stay inside these ranges and needn't reach their ends.
Inputs may be any that keep to these rules, and one draw needn't show every extreme that they name: `stretch_order`: each block's 7 entries are a permutation of 0 .. 6.
All inputs are finite; a program needn't handle non-finite values.
Results may differ from the reference program's by a relative error of at most 0.0004.
Values sent between devices are 32-bit elements; how exact they have to be, the bound alone decides.
A program may use at most 128 MiB of HBM per device.

```python
import math
import jax
import jax.numpy as jnp
from jax import lax

D = 128
TOK_DEV = 896
STRETCH = 128
STRETCHES = 7
WINDOW = 2688
GROUPS = 8
CYCLE_TOKENS = 28672
CYCLE_STRETCHES = 224
TOKENS = 229376


def shared_base(key):
    return jnp.clip(jax.random.normal(key, (GROUPS, CYCLE_TOKENS, D), jnp.float32), -4.0, 4.0)


def draw_keys(key, part):
    base = shared_base(key)
    return base


def draw_queries(key, part):
    key = jax.random.fold_in(key, 21)
    own = jnp.clip(jax.random.normal(key, (GROUPS, CYCLE_TOKENS, D), jnp.float32), -4.0, 4.0)
    return own


def draw_values(key, part):
    key = jax.random.fold_in(key, 31)
    first_key = jax.random.fold_in(key, 1)
    base = jnp.clip(jax.random.normal(first_key, (GROUPS, CYCLE_TOKENS, D), jnp.float32), -4.0, 4.0)
    return base


def draw_stretch_order(key, part):
    key = jax.random.fold_in(key, 41)
    count = GROUPS * (CYCLE_STRETCHES // STRETCHES)
    subkeys = jax.random.split(key, count)
    orders = jax.vmap(lambda single: jax.random.permutation(single, STRETCHES))(subkeys)
    return orders.astype(jnp.int32).reshape(GROUPS, CYCLE_STRETCHES)


def block_scale(key, dims, cuts, low, largest):
    def one(dim, parts):
        heights = jax.random.uniform(jax.random.fold_in(jax.random.fold_in(key, 6), dim), (parts,), jnp.float32, low / len(cuts), largest / len(cuts))
        return jnp.repeat(jnp.exp(heights), dims[dim] // parts).reshape((-1,) + (1,) * (len(dims) - dim - 1))

    level = one(*cuts[0])
    for cut in cuts[1:]:
        level = level * one(*cut)
    return level


def normal_values(stream_key, shape, scale, limit, shards=(), held_as=jnp.bfloat16):
    values = jax.random.normal(stream_key, shape, jnp.float32) * scale
    if len(shards) > 0:
        values = block_scale(stream_key, shape, shards, -0.22, 0.18) * values
    return jnp.clip(values, min=-limit, max=limit).astype(held_as)


def setup_inputs(seed: int = 0) -> dict:
    splits = jax.random.split(jax.random.key(seed), 6)
    return {
        "queries": draw_queries(jax.random.fold_in(splits[5], 71), 0),
        "keys": draw_keys(jax.random.fold_in(splits[5], 71), 0),
        "values": draw_values(jax.random.fold_in(splits[5], 71), 0),
        "out_grad": normal_values(splits[3], (GROUPS, CYCLE_TOKENS, D), 1.0, 6.0, ((0, 8), (1, 32)), jnp.float32),
        "stretch_order": draw_stretch_order(jax.random.fold_in(splits[5], 71), 0),
    }


def matmul(left, right):
    return jnp.dot(left, right, precision=lax.Precision.HIGHEST, preferred_element_type=jnp.float32)

def matmul_nt(left, right):
    return lax.dot_general(left, right, (((1,), (1,)), ((), ())), precision=lax.Precision.HIGHEST, preferred_element_type=jnp.float32)

def matmul_tn(left, right):
    return lax.dot_general(left, right, (((0,), (0,)), ((), ())), precision=lax.Precision.HIGHEST, preferred_element_type=jnp.float32)

def token_positions(stretch_order):
    blocks = TOKENS // TOK_DEV
    order = stretch_order.reshape(blocks, STRETCHES).astype(jnp.int32)
    starts = (jnp.arange(blocks, dtype=jnp.int32) * TOK_DEV)[:, None, None]
    within = jnp.arange(STRETCH, dtype=jnp.int32)[None, None, :]
    return (starts + order[:, :, None] * STRETCH + within).reshape(-1).astype(jnp.int32)

def window_mask(query_pos, key_pos):
    differ = query_pos[:, None] - key_pos[None, :]
    return jnp.logical_and(differ >= 0, differ < WINDOW)

def reference(queries, keys, values, out_grad, stretch_order):
    width = queries.shape[-1]
    scale = 1.0 / math.sqrt(width)
    query_flat = queries.reshape(-1, width)
    key_flat = keys.reshape(-1, width)
    value_flat = values.reshape(-1, width)
    grad_flat = out_grad.reshape(-1, width)
    positions = token_positions(stretch_order)
    blocks = TOKENS // TOK_DEV
    reach = WINDOW
    span = WINDOW + TOK_DEV
    block_ids = jnp.arange(blocks, dtype=jnp.int32)
    key_pad = jnp.concatenate([jnp.zeros((reach, width), jnp.float32), key_flat])
    value_pad = jnp.concatenate([jnp.zeros((reach, width), jnp.float32), value_flat])
    kpos_pad = jnp.concatenate([jnp.full((reach,), -reach, jnp.int32), positions])

    def key_window(index):
        start = (index * TOK_DEV).astype(jnp.int32)
        query_blk = lax.dynamic_slice_in_dim(query_flat, start, TOK_DEV, 0)
        query_pos = lax.dynamic_slice_in_dim(positions, start, TOK_DEV, 0)
        key_win = lax.dynamic_slice_in_dim(key_pad, start, span, 0)
        value_win = lax.dynamic_slice_in_dim(value_pad, start, span, 0)
        kpos_win = lax.dynamic_slice_in_dim(kpos_pad, start, span, 0)
        scores = matmul_nt(query_blk, key_win) * scale
        scores = jnp.where(window_mask(query_pos, kpos_win), scores, -jnp.inf)
        return (start, scores, key_win, value_win)

    def forward_block(index):
        start, scores, key_win, value_win = key_window(index)
        top = lax.optimization_barrier(jnp.max(scores, axis=1))
        weights = jnp.exp(scores - top[:, None])
        total = lax.optimization_barrier(jnp.sum(weights, axis=1))
        output = matmul(weights, value_win) / total[:, None]
        return (output, top + jnp.log(total))
    outputs, lses = lax.map(forward_block, block_ids)
    attn_flat = outputs.reshape(-1, width)
    lse_flat = lses.reshape(-1)
    delta = lax.optimization_barrier(jnp.sum(grad_flat * attn_flat, axis=1))

    def query_block(index):
        start, scores, key_win, value_win = key_window(index)
        lse_blk = lax.dynamic_slice_in_dim(lse_flat, start, TOK_DEV, 0)
        delta_blk = lax.dynamic_slice_in_dim(delta, start, TOK_DEV, 0)
        grad_blk = lax.dynamic_slice_in_dim(grad_flat, start, TOK_DEV, 0)
        probs = jnp.exp(scores - lse_blk[:, None])
        dprobs = matmul_nt(grad_blk, value_win)
        dscores = probs * (dprobs - delta_blk[:, None])
        return matmul(dscores, key_win) * scale
    query_grad = lax.map(query_block, block_ids).reshape(-1, width)
    query_pad = jnp.concatenate([query_flat, jnp.zeros((reach, width), jnp.float32)])
    grad_pad = jnp.concatenate([grad_flat, jnp.zeros((reach, width), jnp.float32)])
    qpos_pad = jnp.concatenate([positions, jnp.full((reach,), TOKENS + 2 * reach, jnp.int32)])
    lse_pad = jnp.concatenate([lse_flat, jnp.zeros((reach,), jnp.float32)])
    delta_pad = jnp.concatenate([delta, jnp.zeros((reach,), jnp.float32)])

    def key_block(index):
        start = (index * TOK_DEV).astype(jnp.int32)
        key_blk = lax.dynamic_slice_in_dim(key_flat, start, TOK_DEV, 0)
        value_blk = lax.dynamic_slice_in_dim(value_flat, start, TOK_DEV, 0)
        kpos_blk = lax.dynamic_slice_in_dim(positions, start, TOK_DEV, 0)
        query_win = lax.dynamic_slice_in_dim(query_pad, start, span, 0)
        grad_win = lax.dynamic_slice_in_dim(grad_pad, start, span, 0)
        qpos_win = lax.dynamic_slice_in_dim(qpos_pad, start, span, 0)
        lse_win = lax.dynamic_slice_in_dim(lse_pad, start, span, 0)
        delta_win = lax.dynamic_slice_in_dim(delta_pad, start, span, 0)
        scores = matmul_nt(query_win, key_blk) * scale
        scores = jnp.where(window_mask(qpos_win, kpos_blk), scores, -jnp.inf)
        probs = jnp.exp(scores - lse_win[:, None])
        value_part = matmul_tn(probs, grad_win)
        dprobs = matmul_nt(grad_win, value_blk)
        dscores = probs * (dprobs - delta_win[:, None])
        key_part = matmul_tn(dscores, query_win) * scale
        return (key_part, value_part)
    key_parts, value_parts = lax.map(key_block, block_ids)
    shape = queries.shape
    return (attn_flat.reshape(shape), query_grad.reshape(shape), key_parts.reshape(shape), value_parts.reshape(shape))
```

```python
import functools
import math

import jax
import jax.numpy as jnp
from jax import lax
from jax.experimental import pallas as pl
from jax.experimental.pallas import tpu as pltpu
from jax.sharding import PartitionSpec as P

F32 = jnp.float32
BF16 = jnp.bfloat16
TOK = 896
D = 128
ST = 128
NS = 7
GROUPS = ((0, 128), (128, 256), (384, 256), (640, 256))
NEG = -1e30
BIG = 1e30
NT = (((1,), (1,)), ((), ()))
NN = (((1,), (0,)), ((), ()))
LOG2E = math.log2(math.e)
MESH = pl.DeviceIdType.MESH


def dot(a, b, dims):
    return lax.dot_general(a, b, dims, preferred_element_type=F32)


def split(x):
    high = x.astype(BF16)
    low = (x - high.astype(F32)).astype(BF16)
    return high, low


def dot_nt(left, right):
    return dot(left, jnp.concatenate([right, right[:, :D]], axis=1), NT)


def dot_nn(x, right):
    high, low = split(x)
    return dot(high, right, NN) + dot(low, right, NN)


def kernel(
    total_devices,
    comm,
    q_ref, k_ref, v_ref, g_ref,
    o_out, dq_out, dk_out, dv_out,
    own, recv,
    own_a, own_b, far_a, mid,
    s0, s1, s2, s3, e0, e1, e2, e3,
    s12, p12, st12, pt12,
    m_acc, l_acc, o_acc, dk_acc, dv_acc,
    lse_c, del_c, stats, stats_in, dsh, dsl,
    send_sem, recv_sem, st_send, st_recv,
):
    s_own = (s0, s1, s2, s3)
    s_far = (e0, e1, e2, e3)
    if comm:
        n_inner = lax.axis_size("inner")
        g = lax.axis_index("outer") * n_inner + lax.axis_index("inner")

        def device(delta):
            t = lax.rem(g + delta + total_devices, total_devices)
            return {"outer": t // n_inner, "inner": lax.rem(t, n_inner)}

        barrier = pltpu.get_barrier_semaphore()
        for delta in (-3, -2, -1, 1, 2, 3):
            pl.semaphore_signal(barrier, inc=1, device_id=device(delta), device_id_type=MESH)
    else:
        g = 5
    par = lax.rem(g, 2)
    sgn = 1 - 2 * par

    own[0, 0] = k_ref[0]
    own[0, 1] = v_ref[0]
    own[1, 0] = q_ref[0] * (LOG2E / math.sqrt(D))
    own[1, 1] = g_ref[0]

    def copy(src, dst, u, delta, send, rsem):
        r0, n = GROUPS[u] if isinstance(u, int) else (pl.multiple_of(256 * u - 128, 128), 256)
        return pltpu.make_async_remote_copy(
            src_ref=src.at[:, pl.ds(r0, n), :],
            dst_ref=dst.at[:, pl.ds(r0, n), :],
            send_sem=send, recv_sem=rsem,
            device_id=device(delta), device_id_type=MESH,
        )

    def make(kind, u):
        if kind == 0:
            return copy(own.at[1 - par], recv.at[1 - par, 0], u, -sgn, send_sem.at[0, u], recv_sem.at[1 - par, 0, u])
        if kind == 1:
            return copy(own.at[par], recv.at[par, 1], u, 2 * sgn, send_sem.at[1, u], recv_sem.at[par, 1, u])
        if kind == 2:
            return copy(own.at[par], recv.at[par, 0], u, sgn, send_sem.at[2, u], recv_sem.at[par, 0, u])
        if kind == 3:
            return copy(recv.at[par, 0], recv.at[par, 1], u, sgn, send_sem.at[3, u], recv_sem.at[par, 1, u])
        if kind == 4:
            return copy(recv.at[par, 0], recv.at[par, 2], u, 2 * sgn, send_sem.at[4, u], recv_sem.at[par, 2, u])
        return copy(recv.at[par, 1], recv.at[par, 2], u, sgn, send_sem.at[5, u], recv_sem.at[par, 2, u])

    def arrived(a, d, u):
        copy(own.at[a], recv.at[a, d], u, 1, send_sem.at[0, u], recv_sem.at[a, d, u]).wait_recv()

    if comm:
        pl.semaphore_wait(barrier, 6)
        for u in range(4):
            make(0, u).start()
            make(1, u).start()
            make(2, u).start()

    def near(u):
        if not comm:
            return
        arrived(par, 0, u)
        make(3, u).start()
        make(4, u).start()
        arrived(par, 1, u)
        make(5, u).start()
        arrived(1 - par, 0, u)
        arrived(1 - par, 1, u)

    for a in range(2):
        for w in range(2):
            high, low = split(own[a, w])
            own_a[a, w, :, 0:D] = high
            own_a[a, w, :, D:2 * D] = low
            own_b[a, w, :, 0:D] = high
            own_b[a, w, :, D:2 * D] = high
            own_b[a, w, :, 2 * D:3 * D] = low

    m_acc[...] = jnp.full_like(m_acc, NEG)
    l_acc[...] = jnp.zeros_like(l_acc)
    o_acc[...] = jnp.zeros_like(o_acc)
    dk_acc[...] = jnp.zeros_like(dk_acc)
    dv_acc[...] = jnp.zeros_like(dv_acc)

    def diag(n, strict):
        row = lax.broadcasted_iota(jnp.int32, (n, n), 0)
        col = lax.broadcasted_iota(jnp.int32, (n, n), 1)
        return (row, col)

    def q_tile(r0, n, ka, va, store, valid, mask):
        rows = slice(r0, r0 + n)
        width = ka.shape[0]
        s = mask(dot_nt(own_b[1, 0, rows, :], ka))
        store[...] = s
        top = s[:, :D] if width == D else jnp.maximum(s[:, :D], s[:, D:])
        top = jnp.max(top, axis=1, keepdims=True)
        old = m_acc[rows, :]
        if valid is not None:
            top = jnp.where(valid, top, NEG)
        new = jnp.maximum(old, top)
        use = new if valid is None else jnp.where(valid, new, BIG)
        alpha = jnp.exp2(old - new)
        m_acc[rows, :] = new
        halves = []
        total = l_acc[rows, :] * alpha
        for h in range(width // D):
            e = jnp.exp2(s[:, h * D:(h + 1) * D] - use)
            total = total + e
            halves.append(e)
        l_acc[rows, :] = total
        e = halves[0] if width == D else jnp.concatenate(halves, axis=1)
        add = dot_nn(e, va)
        o_acc[rows, 0:D] = o_acc[rows, 0:D] * alpha + add[:, 0:D]
        o_acc[rows, D:2 * D] = o_acc[rows, D:2 * D] * alpha + add[:, D:2 * D]

    def same(s):
        return s

    def own_mask(n):
        def mask(s):
            if s.shape[0] == n:
                top, rest = s, None
            else:
                top, rest = s[:n], s[n:]
            row = lax.broadcasted_iota(jnp.int32, (n, n), 0)
            col = lax.broadcasted_iota(jnp.int32, (n, n), 1)
            top = jnp.where(col <= row, top, NEG)
            return top if rest is None else jnp.concatenate([top, rest], axis=0)
        return mask

    def far_mask(n):
        def mask(s):
            m = s.shape[0] - n
            row = lax.broadcasted_iota(jnp.int32, (n, n), 0)
            col = lax.broadcasted_iota(jnp.int32, (n, n), 1)
            last = jnp.where(col > row, s[m:], NEG)
            return last if m == 0 else jnp.concatenate([s[:m], last], axis=0)
        return mask

    for u, (r0, n) in enumerate(GROUPS):
        q_tile(r0, TOK - r0, own_a[0, 0, r0:r0 + n, :], own_a[0, 1, r0:r0 + n, :], s_own[u], None, own_mask(n))

    def put(t, half, a, d, r0, n):
        for w in range(2):
            high, low = split(recv[a, d, w, pl.ds(r0, n), :])
            mid[a, w, t, half:half + n, 0:D] = high
            mid[a, w, t, half:half + n, D:2 * D] = low

    def tile(t, valid, mask):
        q_tile(0, TOK, mid[0, 0, t], mid[0, 1, t], s12.at[t], valid, mask)
        p12[t] = dot_nt(own_b[1, 1], mid[0, 1, t])
        st12[t] = dot_nt(own_b[0, 0], mid[1, 0, t])
        pt12[t] = dot_nt(own_b[0, 1], mid[1, 1, t])

    near(0)
    for a in range(2):
        put(0, 0, a, 0, 0, ST)
        put(0, ST, a, 1, 0, ST)

    def both(s):
        return jnp.concatenate([jnp.where(g >= 1, s[:, :D], NEG), jnp.where(g >= 2, s[:, D:], NEG)], axis=1)

    tile(0, None, both)

    def step(u, carry):
        near(u)
        r0 = pl.multiple_of(256 * u - 128, 128)
        for d in range(2):
            t = 2 * u - 1 + d
            for a in range(2):
                put(t, 0, a, d, r0, 256)
            tile(t, g >= d + 1, same)
        return carry

    lax.fori_loop(1, 4, step, 0)

    def keys_side(q_rows, lse, dlt, scores, dprobs, ga, qa, rows):
        pt = jnp.exp2(scores - lse)
        dv_acc[rows, :] += dot_nn(pt, ga)
        dk_acc[rows, :] += dot_nn(pt * (dprobs - dlt), qa)

    for u in (3, 2, 1, 0):
        r0, n = GROUPS[u]
        rows = slice(r0, r0 + n)
        if comm:
            arrived(0, 2, u)
        for w in range(2):
            high, low = split(recv[0, 2, w, rows, :])
            far_a[0, w, rows, 0:D] = high
            far_a[0, w, rows, D:2 * D] = low
        q_tile(0, r0 + n, far_a[0, 0, rows, :], far_a[0, 1, rows, :], s_far[u], g >= 3, far_mask(n))
        total = jnp.sum(l_acc[rows, :], axis=1, keepdims=True)
        out = (o_acc[rows, 0:D] + o_acc[rows, D:2 * D]) / total
        o_acc[rows, 0:D] = out
        delta = jnp.sum(own[1, 1, rows, :] * out, axis=1, keepdims=True)
        lse = m_acc[rows, :] + jnp.log2(total)
        delta = jnp.broadcast_to(delta, (n, D))
        for j in range(n // ST):
            part = slice(j * ST, (j + 1) * ST)
            cols = slice(r0 + j * ST, r0 + (j + 1) * ST)
            stats[0, :, cols] = jnp.transpose(lse[part])[0:8]
            stats[1, :, cols] = jnp.transpose(delta[part])[0:8]

        def stat_copy(d):
            return pltpu.make_async_remote_copy(
                src_ref=stats.at[:, :, pl.ds(r0, n)],
                dst_ref=stats_in.at[d, :, :, pl.ds(r0, n)],
                send_sem=st_send.at[d, u], recv_sem=st_recv.at[d, u],
                device_id=device(-(d + 1)), device_id_type=MESH,
            )

        if comm:
            for d in range(3):
                stat_copy(d).start()
            arrived(1, 2, u)
        for w in range(2):
            high, low = split(recv[1, 2, w, rows, :])
            far_a[1, w, rows, 0:D] = high
            far_a[1, w, rows, D:2 * D] = low

        def ds_part(s, dp, use):
            return split(jnp.exp2(s - use) * (dp - delta[:, :1]))

        lse1 = lse[:, :1]
        for t in range(7):
            if t == 0:
                use = lse1
            else:
                use = jnp.where(g >= 1 + (t - 1) % 2, lse1, BIG)
            high, low = ds_part(s12[t, rows, :], p12[t, rows, :], use)
            dsh[0:n, t * 256:(t + 1) * 256] = high
            dsl[0:n, t * 256:(t + 1) * 256] = low
        k12 = mid[0, 0].reshape(7 * 256, 256)
        dq = dot(dsh[0:n, :], k12, NN) + dot(dsl[0:n, :], k12, NN)
        for v, (c0, w) in enumerate(GROUPS):
            cols = slice(c0, c0 + w)
            if v <= u:
                s = s_own[v][r0 - c0:r0 - c0 + n, :]
                dp = dot_nt(own_b[1, 1, rows, :], own_a[0, 1, cols, :])
                high, low = ds_part(s, dp, lse1)
                ka = own_a[0, 0, cols, :]
                dq = dq + dot(high, ka, NN) + dot(low, ka, NN)
            if v >= u:
                s = s_far[v][rows, :]
                dp = dot_nt(own_b[1, 1, rows, :], far_a[0, 1, cols, :])
                high, low = ds_part(s, dp, jnp.where(g >= 3, lse1, BIG))
                ka = far_a[0, 0, cols, :]
                dq = dq + dot(high, ka, NN) + dot(low, ka, NN)
        dq_out[0, rows, :] = (dq[:, :D] + dq[:, D:]) * (1.0 / math.sqrt(D))

        m = r0 + n
        ka = own_a[1, 0, rows, :]
        ga = own_a[1, 1, rows, :]
        scores = dot_nt(own_b[0, 0, 0:m, :], ka)
        row = lax.broadcasted_iota(jnp.int32, (n, n), 0)
        col = lax.broadcasted_iota(jnp.int32, (n, n), 1)
        last = jnp.where(row <= col, scores[m - n:], NEG)
        scores = last if m == n else jnp.concatenate([scores[:m - n], last], axis=0)
        dprobs = dot_nt(own_b[0, 1, 0:m, :], ga)
        keys_side(rows, stats[0, 0:1, rows], stats[1, 0:1, rows], scores, dprobs, ga, ka, slice(0, m))
        ka = far_a[1, 0, rows, :]
        ga = far_a[1, 1, rows, :]
        scores = dot_nt(own_b[0, 0, r0:TOK, :], ka)
        first = jnp.where(row > col, scores[:n], NEG)
        scores = first if r0 + n == TOK else jnp.concatenate([first, scores[n:]], axis=0)
        dprobs = dot_nt(own_b[0, 1, r0:TOK, :], ga)
        if comm:
            for d in range(3):
                stat_copy(d).wait_recv()
        last_dev = total_devices - 1
        use = jnp.where(g + 3 <= last_dev, stats_in[2, 0, 0:1, rows], BIG)
        keys_side(rows, use, stats_in[2, 1, 0:1, rows], scores, dprobs, ga, ka, slice(r0, TOK))
        lses = [jnp.where(g + 1 + d <= last_dev, stats_in[d, 0, 0:1, rows], BIG) for d in range(2)]
        dels = [stats_in[d, 1, 0:1, rows] for d in range(2)]
        if u == 0:
            keys_side(
                rows, jnp.concatenate(lses, axis=1), jnp.concatenate(dels, axis=1),
                st12[0], pt12[0], mid[1, 1, 0], mid[1, 0, 0], slice(0, TOK),
            )
        else:
            for d in range(2):
                t = 2 * u - 1 + d
                keys_side(rows, lses[d], dels[d], st12[t], pt12[t], mid[1, 1, t], mid[1, 0, t], slice(0, TOK))

    o_out[0] = o_acc[:, 0:D]
    dk_out[0] = (dk_acc[:, 0:D] + dk_acc[:, D:2 * D]) * (1.0 / LOG2E)
    dv_out[0] = dv_acc[:, 0:D] + dv_acc[:, D:2 * D]

    if comm:
        for u in range(4):
            for kind in range(6):
                make(kind, u).wait_send()
            r0, n = GROUPS[u]
            for d in range(3):
                pltpu.make_async_remote_copy(
                    src_ref=stats.at[:, :, pl.ds(r0, n)],
                    dst_ref=stats_in.at[d, :, :, pl.ds(r0, n)],
                    send_sem=st_send.at[d, u], recv_sem=st_recv.at[d, u],
                    device_id=device(-(d + 1)), device_id_type=MESH,
                ).wait_send()


def place(order_ref, c):
    return pl.multiple_of(order_ref[0, c] * ST, ST)


def sort_kernel(order_ref, *refs):
    for c in range(NS):
        for src, dst in zip(refs[:4], refs[4:]):
            dst[0, pl.ds(place(order_ref, c), ST), :] = src[0, c * ST:(c + 1) * ST, :]


def unsort_kernel(order_ref, *refs):
    for c in range(NS):
        for src, dst in zip(refs[:4], refs[4:]):
            dst[0, c * ST:(c + 1) * ST, :] = src[0, pl.ds(place(order_ref, c), ST), :]


def attention(total_devices, comm, queries, keys, values, out_grad, stretch_order):
    vmem = pl.BlockSpec(memory_space=pltpu.VMEM)
    smem = pl.BlockSpec(memory_space=pltpu.SMEM)
    blk = jax.ShapeDtypeStruct((1, TOK, D), F32)
    own_sizes = [(TOK - r0, n) for r0, n in GROUPS]
    far_sizes = [(r0 + n, n) for r0, n in GROUPS]
    V = pltpu.VMEM
    scratch = [
        V((2, 2, TOK, D), F32), V((2, 3, 2, TOK, D), F32),
        V((2, 2, TOK, 2 * D), BF16), V((2, 2, TOK, 3 * D), BF16), V((2, 2, TOK, 2 * D), BF16),
        V((2, 2, 7, 256, 2 * D), BF16),
    ]
    scratch += [V(s, F32) for s in own_sizes] + [V(s, F32) for s in far_sizes]
    scratch += [V((7, TOK, 256), F32)] * 4
    scratch += [V((TOK, D), F32)] * 2 + [V((TOK, 2 * D), F32)] * 3
    scratch += [V((8, 128), F32)] * 2
    scratch += [V((2, 8, TOK), F32), V((3, 2, 8, TOK), F32)]
    scratch += [V((256, 7 * 256), BF16)] * 2
    scratch += [
        pltpu.SemaphoreType.DMA((6, 4)), pltpu.SemaphoreType.DMA((2, 3, 4)),
        pltpu.SemaphoreType.DMA((3, 4)), pltpu.SemaphoreType.DMA((3, 4)),
    ]
    params = dict(vmem_limit_bytes=63 * 2**20)
    if comm:
        params.update(collective_id=0, has_side_effects=True)
    def reorder(body, name, arrays):
        return pl.pallas_call(
            body, out_shape=[blk] * 4, in_specs=[smem] + [vmem] * 4, out_specs=[vmem] * 4, name=name,
        )(stretch_order, *arrays)

    ordered = reorder(sort_kernel, "by_position", (queries, keys, values, out_grad))
    results = pl.pallas_call(
        functools.partial(kernel, total_devices, comm),
        out_shape=[blk] * 4,
        in_specs=[vmem] * 4,
        out_specs=[vmem] * 4,
        scratch_shapes=scratch,
        compiler_params=pltpu.CompilerParams(**params),
        name="windowed_attention",
    )(*ordered)
    return reorder(unsort_kernel, "by_array", results)


def solution(mesh):
    spec = P("outer", "inner", None)
    total = mesh.shape["outer"] * mesh.shape["inner"]
    return jax.shard_map(
        functools.partial(attention, total, True), mesh=mesh,
        in_specs=(spec, spec, spec, spec, P("outer", "inner")),
        out_specs=(spec,) * 4, check_vma=False,
    )
```

```python
import functools
import math

import jax
import jax.numpy as jnp
from jax import lax
from jax.experimental import pallas as pl
from jax.experimental.pallas import tpu as pltpu
from jax.sharding import PartitionSpec as P

F32 = jnp.float32
BF16 = jnp.bfloat16
TOK = 896
D = 128
ST = 128
NS = 7
GROUPS = ((0, 128), (128, 256), (384, 256), (640, 256))
NEG = -1e30
BIG = 1e30
NT = (((1,), (1,)), ((), ()))
NN = (((1,), (0,)), ((), ()))
LOG2E = math.log2(math.e)
MESH = pl.DeviceIdType.MESH


def dot(a, b, dims):
    return lax.dot_general(a, b, dims, preferred_element_type=F32)


def split(x):
    high = x.astype(BF16)
    low = (x - high.astype(F32)).astype(BF16)
    return high, low


def dot_nt(left, right):
    return dot(left, jnp.concatenate([right, right[:, :D]], axis=1), NT)


def dot_nn(x, right):
    high, low = split(x)
    return dot(high, right, NN) + dot(low, right, NN)


def kernel(
    total_devices,
    comm,
    order_ref, q_hbm, k_hbm, v_hbm, g_hbm,
    o_hbm, dq_hbm, dk_hbm, dv_hbm,
    stage, own, recv,
    own_a, own_b, far_a, mid,
    s0, s1, s2, s3, e0, e1, e2, e3,
    p0, p1, p2, p3, st0, st1, st2, st3, pt0, pt1, pt2, pt3,
    s12, p12, st12, pt12,
    m_acc, l_acc, o_acc, dk_acc, dv_acc,
    lse_c, del_c, stats, stats_in, dsh, dsl,
    send_sem, recv_sem, st_send, st_recv, in_sem, out_sem,
):
    s_own = (s0, s1, s2, s3)
    s_far = (e0, e1, e2, e3)
    p_own = (p0, p1, p2, p3)
    st_own = (st0, st1, st2, st3)
    pt_own = (pt0, pt1, pt2, pt3)
    if comm:
        n_inner = lax.axis_size("inner")
        g = lax.axis_index("outer") * n_inner + lax.axis_index("inner")

        def device(delta):
            t = lax.rem(g + delta + total_devices, total_devices)
            return {"outer": t // n_inner, "inner": lax.rem(t, n_inner)}

        def inside(*deltas):
            low, high = min(deltas), max(deltas)
            return jnp.logical_and(g + low >= 0, g + high < total_devices)

        barrier = pltpu.get_barrier_semaphore()

        def greet(delta):
            pl.semaphore_signal(barrier, inc=1, device_id=device(delta), device_id_type=MESH)

        for delta in (-3, -2, -1, 1, 2, 3):
            pl.when(inside(delta))(functools.partial(greet, delta))
    else:
        g = 5
    par = lax.rem(g, 2)
    sgn = 1 - 2 * par

    loads = [
        pltpu.make_async_copy(ref, stage.at[i], in_sem.at[i])
        for i, ref in enumerate((k_hbm, v_hbm, q_hbm, g_hbm))
    ]
    for load in loads:
        load.start()

    def source(s):
        total = 0
        unit = 1
        for k in range(NS):
            if k != s:
                unit = unit * (s - k)
        for c in range(1, NS):
            term = c
            for k in range(NS):
                if k != s:
                    term = term * (order_ref[0, c] - k)
            total = total + term
        return lax.rem(lax.div(total, jnp.int32(unit)), jnp.int32(NS))

    places = [source(s) for s in range(NS)]
    for load in loads:
        load.wait()
    for s in range(NS):
        rows = slice(s * ST, (s + 1) * ST)
        own[0, 0, rows, :] = stage[0, places[s]]
        own[0, 1, rows, :] = stage[1, places[s]]
        own[1, 0, rows, :] = stage[2, places[s]] * (LOG2E / math.sqrt(D))
        own[1, 1, rows, :] = stage[3, places[s]]

    def copy(src, dst, u, delta, send, rsem):
        r0, n = GROUPS[u] if isinstance(u, int) else (pl.multiple_of(256 * u - 128, 128), 256)
        return pltpu.make_async_remote_copy(
            src_ref=src.at[:, pl.ds(r0, n), :],
            dst_ref=dst.at[:, pl.ds(r0, n), :],
            send_sem=send, recv_sem=rsem,
            device_id=device(delta), device_id_type=MESH,
        )

    def make(kind, u):
        if kind == 0:
            return copy(own.at[1 - par], recv.at[1 - par, 0], u, -sgn, send_sem.at[0, u], recv_sem.at[1 - par, 0, u])
        if kind == 1:
            return copy(own.at[par], recv.at[par, 1], u, 2 * sgn, send_sem.at[1, u], recv_sem.at[par, 1, u])
        if kind == 2:
            return copy(own.at[par], recv.at[par, 0], u, sgn, send_sem.at[2, u], recv_sem.at[par, 0, u])
        if kind == 3:
            return copy(recv.at[par, 0], recv.at[par, 1], u, sgn, send_sem.at[3, u], recv_sem.at[par, 1, u])
        if kind == 4:
            return copy(recv.at[par, 0], recv.at[par, 2], u, 2 * sgn, send_sem.at[4, u], recv_sem.at[par, 2, u])
        return copy(recv.at[par, 1], recv.at[par, 2], u, sgn, send_sem.at[5, u], recv_sem.at[par, 2, u])

    def exists(kind):
        carried, to = ((0, -1), (0, 2), (0, 1), (-1, 1), (-1, 2), (-2, 1))[kind]
        first, second = g + sgn * carried, g + sgn * to
        return jnp.logical_and(
            jnp.minimum(first, second) >= 0, jnp.maximum(first, second) < total_devices
        )

    def start(*which):
        for kind, u in which:
            pl.when(exists(kind))(make(kind, u).start)

    def wait_sent(kind, u):
        pl.when(exists(kind))(make(kind, u).wait_send)

    def arrived(a, d, u):
        block = g + (2 * a - 1) * (d + 1)
        here = jnp.logical_and(block >= 0, block < total_devices)
        pl.when(here)(
            copy(own.at[a], recv.at[a, d], u, 1, send_sem.at[0, u], recv_sem.at[a, d, u]).wait_recv
        )

    if comm:
        pl.semaphore_wait(barrier, jnp.minimum(g, 3) + jnp.minimum(total_devices - 1 - g, 3))
        for u in (0, 3):
            start((0, u), (1, u))
        start((2, 0), (2, 3), (2, 2), (2, 1))

    def near(u):
        if not comm:
            return
        arrived(par, 0, u)
        start((3, u))
        if isinstance(u, int):
            start((0, 2), (1, 2))
        else:
            pl.when(u == 3)(lambda: start((0, 1), (1, 1)))
            pl.when(u == 2)(lambda: start((4, 3)))
            pl.when(u == 1)(lambda: start((4, 2)))
        arrived(par, 1, u)
        start((5, u))
        arrived(1 - par, 0, u)

    def last_near(u):
        if comm:
            arrived(1 - par, 1, u)

    for a in range(2):
        for w in range(2):
            high, low = split(own[a, w])
            own_a[a, w, :, 0:D] = high
            own_a[a, w, :, D:2 * D] = low
            own_b[a, w, :, 0:D] = high
            own_b[a, w, :, D:2 * D] = high
            own_b[a, w, :, 2 * D:3 * D] = low

    if comm:
        def clear(a, d):
            recv[a, d] = jnp.zeros((2, TOK, D), F32)

        for d in range(3):
            pl.when(g < d + 1)(functools.partial(clear, 0, d))
            pl.when(g > total_devices - 2 - d)(functools.partial(clear, 1, d))

    m_acc[...] = jnp.full_like(m_acc, NEG)
    l_acc[...] = jnp.zeros_like(l_acc)
    o_acc[...] = jnp.zeros_like(o_acc)
    dk_acc[...] = jnp.zeros_like(dk_acc)
    dv_acc[...] = jnp.zeros_like(dv_acc)

    def diag(n, strict):
        row = lax.broadcasted_iota(jnp.int32, (n, n), 0)
        col = lax.broadcasted_iota(jnp.int32, (n, n), 1)
        return (row, col)

    def q_tile(r0, n, ka, va, store, valid, mask):
        rows = slice(r0, r0 + n)
        width = ka.shape[0]
        s = mask(dot_nt(own_b[1, 0, rows, :], ka))
        store[...] = s
        top = s[:, :D] if width == D else jnp.maximum(s[:, :D], s[:, D:])
        top = jnp.max(top, axis=1, keepdims=True)
        old = m_acc[rows, :]
        if valid is not None:
            top = jnp.where(valid, top, NEG)
        new = jnp.maximum(old, top)
        use = new if valid is None else jnp.where(valid, new, BIG)
        alpha = jnp.exp2(old - new)
        m_acc[rows, :] = new
        halves = []
        total = l_acc[rows, :] * alpha
        for h in range(width // D):
            e = jnp.exp2(s[:, h * D:(h + 1) * D] - use)
            total = total + e
            halves.append(e)
        l_acc[rows, :] = total
        e = halves[0] if width == D else jnp.concatenate(halves, axis=1)
        add = dot_nn(e, va)
        o_acc[rows, 0:D] = o_acc[rows, 0:D] * alpha + add[:, 0:D]
        o_acc[rows, D:2 * D] = o_acc[rows, D:2 * D] * alpha + add[:, D:2 * D]

    def same(s):
        return s

    def own_mask(n):
        def mask(s):
            if s.shape[0] == n:
                top, rest = s, None
            else:
                top, rest = s[:n], s[n:]
            row = lax.broadcasted_iota(jnp.int32, (n, n), 0)
            col = lax.broadcasted_iota(jnp.int32, (n, n), 1)
            top = jnp.where(col <= row, top, NEG)
            return top if rest is None else jnp.concatenate([top, rest], axis=0)
        return mask

    def far_mask(n):
        def mask(s):
            m = s.shape[0] - n
            row = lax.broadcasted_iota(jnp.int32, (n, n), 0)
            col = lax.broadcasted_iota(jnp.int32, (n, n), 1)
            last = jnp.where(col > row, s[m:], NEG)
            return last if m == 0 else jnp.concatenate([s[:m], last], axis=0)
        return mask

    for u, (r0, n) in enumerate(GROUPS):
        q_tile(r0, TOK - r0, own_a[0, 0, r0:r0 + n, :], own_a[0, 1, r0:r0 + n, :], s_own[u], None, own_mask(n))

        p_own[u][...] = dot_nt(own_b[1, 1, r0:TOK, :], own_a[0, 1, r0:r0 + n, :])
    for u, (r0, n) in enumerate(GROUPS):
        m = r0 + n
        row = lax.broadcasted_iota(jnp.int32, (n, n), 0)
        col = lax.broadcasted_iota(jnp.int32, (n, n), 1)
        scores = dot_nt(own_b[0, 0, 0:m, :], own_a[1, 0, r0:m, :])
        last = jnp.where(row <= col, scores[r0:], NEG)
        st_own[u][...] = last if r0 == 0 else jnp.concatenate([scores[:r0], last], axis=0)
        pt_own[u][...] = dot_nt(own_b[0, 1, 0:m, :], own_a[1, 1, r0:m, :])

    def put(t, half, a, d, r0, n):
        for w in range(2):
            high, low = split(recv[a, d, w, pl.ds(r0, n), :])
            mid[a, w, t, half:half + n, 0:D] = high
            mid[a, w, t, half:half + n, D:2 * D] = low

    def tile(t, valid, mask):
        q_tile(0, TOK, mid[0, 0, t], mid[0, 1, t], s12.at[t], valid, mask)
        p12[t] = dot_nt(own_b[1, 1], mid[0, 1, t])
        st12[t] = dot_nt(own_b[0, 0], mid[1, 0, t])
        pt12[t] = dot_nt(own_b[0, 1], mid[1, 1, t])

    def both(s):
        return jnp.concatenate([jnp.where(g >= 1, s[:, :D], NEG), jnp.where(g >= 2, s[:, D:], NEG)], axis=1)

    near(0)
    last_near(0)
    for a in range(2):
        put(0, 0, a, 0, 0, ST)
        put(0, ST, a, 1, 0, ST)
    tile(0, None, both)

    def step(i, carry):
        u = 3 - i
        near(u)
        r0 = pl.multiple_of(256 * u - 128, 128)
        for d in range(2):
            t = 2 * u - 1 + d
            if d == 1:
                last_near(u)
            for a in range(2):
                put(t, 0, a, d, r0, 256)
            tile(t, g >= d + 1, same)
        return carry

    lax.fori_loop(0, 3, step, 0)

    def put_out(i, rows, value):
        for j in range(value.shape[0] // ST):
            stage[i, rows.start // ST + j] = value[j * ST:(j + 1) * ST]

    def query_grad(r0, m):
        end = r0 + m

        def part(s, dp, first, last, valid=None):
            use = m_acc[first:last, 0:1]
            if valid is not None:
                use = jnp.where(valid, use, BIG)
            return split(jnp.exp2(s - use) * (dp - l_acc[first:last, 0:1]))

        for t in range(7):
            valid = None if t == 0 else g >= 1 + (t - 1) % 2
            high, low = part(s12[t, r0:end, :], p12[t, r0:end, :], r0, end, valid)
            dsh[0:m, t * 256:(t + 1) * 256] = high
            dsl[0:m, t * 256:(t + 1) * 256] = low
        k12 = mid[0, 0].reshape(7 * 256, 256)
        o_acc[r0:end, :] = dot(dsh[0:m, :], k12, NN) + dot(dsl[0:m, :], k12, NN)
        for v, (c0, w) in enumerate(GROUPS):
            cols = slice(c0, c0 + w)
            first, last = max(c0, r0), min(c0 + w, end)
            if first < end:
                high, low = part(s_own[v][first - c0:end - c0, :], p_own[v][first - c0:end - c0, :], first, end)
                ka = own_a[0, 0, cols, :]
                o_acc[first:end, :] += dot(high, ka, NN) + dot(low, ka, NN)
            if last > r0:
                dp = dot_nt(own_b[1, 1, r0:last, :], far_a[0, 1, cols, :])
                high, low = part(s_far[v][r0:last, :], dp, r0, last, g >= 3)
                ka = far_a[0, 0, cols, :]
                o_acc[r0:last, :] += dot(high, ka, NN) + dot(low, ka, NN)
        grad = (o_acc[r0:end, 0:D] + o_acc[r0:end, D:2 * D]) * (1.0 / math.sqrt(D))
        put_out(1, slice(r0, end), grad)

    def keys_side(q_rows, lse, dlt, scores, dprobs, ga, qa, rows):
        pt = jnp.exp2(scores - lse)
        dv_acc[rows, :] += dot_nn(pt, ga)
        dk_acc[rows, :] += dot_nn(pt * (dprobs - dlt), qa)

    def stat_copy(d, u):
        r0, n = GROUPS[u]
        return pltpu.make_async_remote_copy(
            src_ref=stats.at[:, :, pl.ds(r0, n)],
            dst_ref=stats_in.at[d, :, :, pl.ds(r0, n)],
            send_sem=st_send.at[d, u], recv_sem=st_recv.at[d, u],
            device_id=device(-(d + 1)), device_id_type=MESH,
        )

    last_dev = total_devices - 1

    def post(u):
        r0, n = GROUPS[u]
        rows = slice(r0, r0 + n)
        if comm:
            for d in range(3):
                pl.when(inside(d + 1))(stat_copy(d, u).wait_recv)
        lses = [jnp.where(g + 1 + d <= last_dev, stats_in[d, 0, 0:1, rows], BIG) for d in range(3)]
        dels = [jnp.where(g + 1 + d <= last_dev, stats_in[d, 1, 0:1, rows], 0.0) for d in range(3)]
        if u == 0:
            keys_side(
                rows, jnp.concatenate(lses[:2], axis=1), jnp.concatenate(dels[:2], axis=1),
                st12[0], pt12[0], mid[1, 1, 0], mid[1, 0, 0], slice(0, TOK),
            )
        else:
            for d in range(2):
                t = 2 * u - 1 + d
                keys_side(rows, lses[d], dels[d], st12[t], pt12[t], mid[1, 1, t], mid[1, 0, t], slice(0, TOK))
        if comm:
            arrived(1, 2, u)
        for w in range(2):
            high, low = split(recv[1, 2, w, rows, :])
            far_a[1, w, rows, 0:D] = high
            far_a[1, w, rows, D:2 * D] = low
        scores = dot_nt(own_b[0, 0, r0:TOK, :], far_a[1, 0, rows, :])
        row = lax.broadcasted_iota(jnp.int32, (n, n), 0)
        col = lax.broadcasted_iota(jnp.int32, (n, n), 1)
        first = jnp.where(row > col, scores[:n], NEG)
        scores = first if r0 + n == TOK else jnp.concatenate([first, scores[n:]], axis=0)
        dprobs = dot_nt(own_b[0, 1, r0:TOK, :], far_a[1, 1, rows, :])
        keys_side(
            rows, lses[2], dels[2], scores, dprobs,
            far_a[1, 1, rows, :], far_a[1, 0, rows, :], slice(r0, TOK),
        )

    for u in (3, 2, 1, 0):
        r0, n = GROUPS[u]
        rows = slice(r0, r0 + n)
        if comm:
            arrived(0, 2, u)
            if u == 3:
                start((4, 1), (4, 0))
        for w in range(2):
            high, low = split(recv[0, 2, w, rows, :])
            far_a[0, w, rows, 0:D] = high
            far_a[0, w, rows, D:2 * D] = low
        q_tile(0, r0 + n, far_a[0, 0, rows, :], far_a[0, 1, rows, :], s_far[u], g >= 3, far_mask(n))
        total = jnp.sum(l_acc[rows, :], axis=1, keepdims=True)
        out = (o_acc[rows, 0:D] + o_acc[rows, D:2 * D]) / total
        put_out(0, rows, out)
        delta = jnp.sum(own[1, 1, rows, :] * out, axis=1, keepdims=True)
        lse = m_acc[rows, :] + jnp.log2(total)
        delta = jnp.broadcast_to(delta, (n, D))
        for j in range(n // ST):
            part = slice(j * ST, (j + 1) * ST)
            cols = slice(r0 + j * ST, r0 + (j + 1) * ST)
            stats[0, :, cols] = jnp.transpose(lse[part])[0:8]
            stats[1, :, cols] = jnp.transpose(delta[part])[0:8]

        if comm:
            for d in range(3):
                pl.when(inside(-(d + 1)))(stat_copy(d, u).start)
        m_acc[rows, :] = lse
        l_acc[rows, :] = delta
        if u % 2 == 0:
            query_grad(r0, 512 if u else 384)

        keys_side(
            rows, stats[0, 0:1, rows], stats[1, 0:1, rows], st_own[u][...], pt_own[u][...],
            own_a[1, 1, rows, :], own_a[1, 0, rows, :], slice(0, r0 + n),
        )

    stores = [
        pltpu.make_async_copy(stage.at[i], ref, out_sem.at[i])
        for i, ref in enumerate((o_hbm, dq_hbm, dk_hbm, dv_hbm))
    ]
    stores[0].start()
    stores[1].start()
    for u in (3, 2, 1, 0):
        post(u)
    put_out(2, slice(0, TOK), (dk_acc[:, 0:D] + dk_acc[:, D:2 * D]) * (1.0 / LOG2E))
    put_out(3, slice(0, TOK), dv_acc[:, 0:D] + dv_acc[:, D:2 * D])
    stores[2].start()
    stores[3].start()

    if comm:
        for u in range(4):
            for kind in range(6):
                wait_sent(kind, u)
            for d in range(3):
                pl.when(inside(-(d + 1)))(stat_copy(d, u).wait_send)
    for store in stores:
        store.wait()


def unsort_kernel(order_ref, *refs):
    for c in range(NS):
        for src, dst in zip(refs[:4], refs[4:]):
            dst[c] = src[order_ref[0, c]]


def attention(total_devices, comm, queries, keys, values, out_grad, stretch_order):
    vmem = pl.BlockSpec(memory_space=pltpu.VMEM)
    smem = pl.BlockSpec(memory_space=pltpu.SMEM)
    blk = jax.ShapeDtypeStruct((NS, ST, D), F32)
    anywhere = pl.BlockSpec(memory_space=pl.ANY)
    own_sizes = [(TOK - r0, n) for r0, n in GROUPS]
    far_sizes = [(r0 + n, n) for r0, n in GROUPS]
    V = pltpu.VMEM
    scratch = [
        V((4, NS, ST, D), F32), V((2, 2, TOK, D), F32), V((2, 3, 2, TOK, D), F32),
        V((2, 2, TOK, 2 * D), BF16), V((2, 2, TOK, 3 * D), BF16), V((2, 2, TOK, 2 * D), BF16),
        V((2, 2, 7, 256, 2 * D), BF16),
    ]
    scratch += [V(s, F32) for s in own_sizes] + [V(s, F32) for s in far_sizes]
    scratch += [V(s, F32) for s in own_sizes + far_sizes + far_sizes]
    scratch += [V((7, TOK, 256), F32)] * 4
    scratch += [V((TOK, D), F32)] * 2 + [V((TOK, 2 * D), F32)] * 3
    scratch += [V((8, 128), F32)] * 2
    scratch += [V((2, 8, TOK), F32), V((3, 2, 8, TOK), F32)]
    scratch += [V((512, 7 * 256), BF16)] * 2
    scratch += [
        pltpu.SemaphoreType.DMA((6, 4)), pltpu.SemaphoreType.DMA((2, 3, 4)),
        pltpu.SemaphoreType.DMA((3, 4)), pltpu.SemaphoreType.DMA((3, 4)),
        pltpu.SemaphoreType.DMA((4,)), pltpu.SemaphoreType.DMA((4,)),
    ]
    params = dict(vmem_limit_bytes=63 * 2**20)
    if comm:
        params.update(collective_id=0, has_side_effects=True)
    results = pl.pallas_call(
        functools.partial(kernel, total_devices, comm),
        out_shape=[blk] * 4,
        in_specs=[smem] + [anywhere] * 4,
        out_specs=[anywhere] * 4,
        scratch_shapes=scratch,
        compiler_params=pltpu.CompilerParams(**params),
        name="windowed_attention",
    )(stretch_order, *(x.reshape(NS, ST, D) for x in (queries, keys, values, out_grad)))
    results = pl.pallas_call(
        unsort_kernel,
        out_shape=[blk] * 4,
        in_specs=[smem] + [vmem] * 4,
        out_specs=[vmem] * 4,
        name="by_array",
    )(stretch_order, *results)
    return tuple(x.reshape(1, TOK, D) for x in results)


def solution(mesh):
    spec = P("outer", "inner", None)
    total = mesh.shape["outer"] * mesh.shape["inner"]
    return jax.shard_map(
        functools.partial(attention, total, True), mesh=mesh,
        in_specs=(spec, spec, spec, spec, P("outer", "inner")),
        out_specs=(spec,) * 4, check_vma=False,
    )
```
